256 devices in a mesh: st: 32 (over x, y, core), ha: 8 (over z).
Axes of the slice: x: 4, y: 4, z: 8, core: 2. Of those that a mesh axis runs over, the one named last changes fastest.
Arguments:
- clip_lengths: int32 [4], replicated, may hold values from 1 to 32, 64 in all
- inst_frame: int32 [4096, 1], P('st'), may hold values from 0 to 63; in each aligned block of 128 rows (0 to 127, 128 to 255, ...) at most 4 rows name the same one
- query_rows: int32 [4096], P('st'), may hold values from 1 to 16
- pix_q: bfloat16 [64, 256, 64, 128], P('st', 'ha'), may hold values from -140 to 140
- pix_k: bfloat16 [64, 256, 64, 128], P('st', 'ha'), may hold values from -4.5 to 4.5
- pix_v: bfloat16 [64, 256, 64, 128], P('st', 'ha'), may hold values from -6 to 6
- features: bfloat16 [64, 256, 64, 128], P('st', 'ha'), may hold values from -4 to 4
- pixel_gain: float32 [256], P('ha'), may hold values from 0.1 to 1.9
- inst_query: bfloat16 [4096, 16, 256], P('st', None, 'ha'), may hold values from -135 to 135
- inst_gain: float32 [256], P('ha'), may hold values from 0.1 to 1.9
Outputs:
- pixel_out: bfloat16 [64, 256, 64, 128], P('st', 'ha')
- inst_out: bfloat16 [4096, 16, 256], P('st', None, 'ha')
The draws below stay inside these ranges and needn't reach their ends.
Inputs may be any that keep to these rules, and one draw needn't show every extreme that they name: `clip_lengths`: the clips lie end to end in frame order and their lengths sum to 64. `inst_frame`: among the instances held by one index of st, no frame is named by more than 4 instances.
All inputs are finite; a program needn't handle non-finite values.
Results may differ from the reference program's by a relative error of at most 0.012.
Values may be sent and summed in bfloat16 or wider, within the bound.
A program may use at most 64 MiB of HBM per device.

```python
import math
from functools import partial
import jax
import jax.numpy as jnp
import numpy as np
from jax import lax

H = 64
W = 128
C = 256
HEADS = 8
HD = 32
INST_DEV = 128
QMAX = 16
FRAMES = 64
CLIPS = 4
CLIP_MOST = 32
FRAME_MOST = 4
INST = 4096


def base_keys(key):
    raw = jax.random.normal(jax.random.fold_in(key, 11), (FRAMES, C, H, W), jnp.float32)
    return jnp.clip(raw, -4.5, 4.5)


def draw_pix_k(key, part):
    return base_keys(key).astype(jnp.bfloat16)


def draw_pix_q(key, part):
    raw = jnp.clip(jax.random.normal(jax.random.fold_in(key, 12), (FRAMES, C, H, W), jnp.float32), -4.5, 4.5)
    return raw.astype(jnp.bfloat16)


def draw_inst_query(key, part):
    raw = jnp.clip(jax.random.normal(jax.random.fold_in(key, 21), (INST, QMAX, C), jnp.float32), -4.5, 4.5)
    return raw.astype(jnp.bfloat16)


def draw_query_rows(key, part):
    counts = jax.random.randint(jax.random.fold_in(key, 31), (INST,), 1, QMAX + 1)
    chosen_row = jax.random.randint(jax.random.fold_in(key, 32), (), 0, INST)
    return counts.at[chosen_row].set(QMAX).astype(jnp.int32)


def shard_levels(stream_key, extent, pieces, smallest, high):
    level, own = 1.0, jax.random.fold_in(stream_key, 6)
    for dim, shards_of in pieces:
        steps = jnp.exp(jax.random.uniform(jax.random.fold_in(own, dim), (shards_of,), jnp.float32, smallest / len(pieces), high / len(pieces)))
        level = level * jnp.repeat(steps, extent[dim] // shards_of).reshape([-1 if axis == dim else 1 for axis in range(len(extent))])
    return level


def profile(number_of, total, most, skew):
    portions = [(1 << 20) // math.isqrt(grade ** skew) + 1 for grade in range(2, number_of + 1)]
    rest, given = total - most - (number_of - 1), [1] * (number_of - 1)
    while rest > 0:
        movable = [i for i in range(number_of - 1) if given[i] < most]
        mass, left = sum([portions[i] for i in movable]), rest
        for i in movable:
            more = min(most - given[i], max(1, left * portions[i] // mass), rest)
            given[i] = given[i] + more
            rest = rest - more
    return np.array([most] + given)


def uneven_parts(rng, count, total, reach, skew):
    if count == 2:
        one = jax.random.randint(rng, (), max(1, total - reach), min(reach, total - 1) + 1)
        return jnp.stack([one, total - one])
    lengths = jnp.asarray(profile(count, total, reach, skew), jnp.int32)
    twos = (count - 1) // 2
    giver, taker = lengths[1:1 + 2 * twos:2], lengths[2:2 + 2 * twos:2]
    slack = jnp.minimum(giver - 1, reach - taker)
    passed = jax.random.randint(jax.random.fold_in(rng, 1), (twos,), 0, 1 << 20) % (slack + 1)
    lengths = lengths.at[1:1 + 2 * twos:2].set(giver - passed).at[2:2 + 2 * twos:2].set(taker + passed)
    return lengths[jax.random.permutation(jax.random.fold_in(rng, 2), count)]


def deal_out(rng, own, number, rows, amount, top, reach, skew):
    order = jax.random.permutation(rng, amount)
    crowded, usual = portions_of(amount, rows * top, reach, skew, True), portions_of(amount, rows * top, reach, skew, False)
    places = jnp.arange(amount)

    def named(sizes, turn):
        used = int((sizes > 0).sum())
        fixed = max(1, used // 4)
        shifted = fixed + (places - fixed + turn * (used - fixed)) % max(1, amount - fixed)
        return jnp.zeros((amount,), jnp.int32).at[order[jnp.where(places < fixed, places, shifted)]].set(jnp.asarray(sizes, jnp.int32))

    sizes = jnp.where(number % 4 == 0, named(crowded, number // 4), named(usual, number - number // 4 - 1))
    mixed = jax.random.permutation(jax.random.fold_in(own, 3), amount)
    giver, sink = mixed[0:amount // 2 * 2:2], mixed[1:amount // 2 * 2:2]
    margin = jnp.minimum(sizes[giver] - 1, reach - sizes[sink]) // 2
    margin = jnp.where((giver == order[0]) | (sink == order[0]) | (sizes[sink] == 0), 0, jnp.maximum(margin, 0))
    shifted = jax.random.randint(jax.random.fold_in(own, 4), (amount // 2,), 0, 1 << 20) % (margin + 1)
    sizes = sizes.at[giver].add(-shifted).at[sink].add(shifted)
    labels = jnp.searchsorted(jnp.cumsum(sizes), jnp.arange(rows * top), side="right").astype(jnp.int32)
    listing = labels.reshape(top, rows).T
    listing = listing[jax.random.permutation(jax.random.fold_in(own, 1), rows)]
    turn = jax.random.randint(jax.random.fold_in(own, 2), (rows, 1), 0, top)
    return jnp.take_along_axis(listing, (jnp.arange(top)[None, :] + turn) % top, axis=1)


def portions_of(amount, total, most, slope, full):
    loads = [(1 << 20) // math.isqrt(grade ** slope) + 1 for grade in range(1, amount + 1)]
    largest = most if full else min(most, max(-(-total // amount), total * loads[0] // sum(loads)))
    least = 1 if total - largest >= amount - 1 else 0
    given, surplus = [largest] + [least] * (amount - 1), total - largest - least * (amount - 1)
    while surplus > 0:
        free = [i for i in range(1, amount) if given[i] < largest] or [i for i in range(1, amount) if given[i] < most]
        whole, budget = sum([loads[i] for i in free]), surplus
        for i in free:
            addition = min(most - given[i], max(1, budget * loads[i] // whole), surplus)
            given[i] = given[i] + addition
            surplus = surplus - addition
    return np.array(given)


def normal_values(rng, extent, deviation, reach, shards=(), held_as=jnp.bfloat16):
    drawn = jax.random.normal(rng, extent, jnp.float32) * deviation
    if len(shards) > 0:
        drawn = shard_levels(rng, extent, shards, -0.22, 0.18) * drawn
    return jnp.clip(drawn, min=-reach, max=reach).astype(held_as)


def setup_inputs(seed: int = 0) -> dict:
    seeds = jax.random.split(jax.random.key(seed), 11)
    clip_lengths = uneven_parts(seeds[0], CLIPS, FRAMES, CLIP_MOST, 2).astype(jnp.int32)
    inst_frame_keys = jax.random.split(jax.random.fold_in(seeds[1], 1), INST // INST_DEV)
    inst_frame_turns = jax.random.permutation(jax.random.fold_in(seeds[1], 3), INST // INST_DEV)
    inst_frame = jax.vmap(lambda own, number: deal_out(jax.random.fold_in(seeds[1], 2), own, number, INST_DEV, FRAMES, 1, FRAME_MOST, 2))(inst_frame_keys, inst_frame_turns).reshape((INST, 1))
    query_rows = draw_query_rows(jax.random.fold_in(seeds[10], 71), 0)
    pix_q = draw_pix_q(jax.random.fold_in(seeds[10], 71), 0)
    pix_k = draw_pix_k(jax.random.fold_in(seeds[10], 71), 0)
    pix_v = normal_values(seeds[5], (FRAMES, C, H, W), 1.0, 6.0, ((0, 32), (1, 8)))
    features = normal_values(seeds[6], (FRAMES, C, H, W), 0.5, 4.0, ((0, 32), (1, 8)))
    pixel_gain = jnp.clip(1.0 + 0.18 * jax.random.normal(seeds[7], (C,), jnp.float32), 0.1, 1.9)
    inst_query = draw_inst_query(jax.random.fold_in(seeds[10], 71), 0)
    inst_gain = jnp.clip(1.0 + 0.18 * jax.random.normal(seeds[9], (C,), jnp.float32), 0.1, 1.9)
    return {"clip_lengths": clip_lengths, "inst_frame": inst_frame, "query_rows": query_rows, "pix_q": pix_q, "pix_k": pix_k, "pix_v": pix_v, "features": features, "pixel_gain": pixel_gain, "inst_query": inst_query, "inst_gain": inst_gain}


EPSILON = 1e-05
MASKED = -1e+30

def soft_weights(scores, axis_num):
    largest = lax.optimization_barrier(jnp.max(scores, axis=axis_num, keepdims=True))
    raised = jnp.exp(scores - largest)
    return (raised / lax.optimization_barrier(jnp.sum(raised, axis=axis_num, keepdims=True))).astype(jnp.bfloat16)

def spatial_frame(inputs):
    query_f, key_f, value_f = inputs
    scale_val = HD ** (-0.5)
    query_h = query_f.astype(jnp.float32).reshape(HEADS, HD, H, W)
    key_h = key_f.astype(jnp.float32).reshape(HEADS, HD, H, W)
    value_h = value_f.astype(jnp.float32).reshape(HEADS, HD, H, W)
    height_scores = jnp.einsum('ndhw,ndgw->nhgw', query_h, key_h) * scale_val
    height_weights = soft_weights(height_scores, 2).astype(jnp.float32)
    height_out = jnp.einsum('nhgw,ndgw->ndhw', height_weights, value_h)
    width_scores = jnp.einsum('ndhw,ndhv->nhwv', query_h, key_h) * scale_val
    width_weights = soft_weights(width_scores, 3).astype(jnp.float32)
    width_out = jnp.einsum('nhwv,ndhv->ndhw', width_weights, value_h)
    return (height_out + width_out).reshape(C, H, W)

def temporal_head(same_clip, inputs):
    query_h, key_h, value_h = inputs
    scale_val = HD ** (-0.5)
    scores = jnp.einsum('fdhw,gdhw->fghw', query_h.astype(jnp.float32), key_h.astype(jnp.float32)) * scale_val
    masked = jnp.where(same_clip[:, :, None, None], scores, MASKED)
    weights = soft_weights(masked, 1).astype(jnp.float32)
    return jnp.einsum('fghw,gdhw->fdhw', weights, value_h.astype(jnp.float32)).astype(jnp.bfloat16)

def by_heads(tensor):
    return jnp.moveaxis(tensor.reshape(FRAMES, HEADS, HD, H, W), 1, 0)

def normalize(values_in, totals, squares, count_all, gain_vec):
    average = totals / count_all
    variance = squares / count_all - average * average
    return (values_in - average) * lax.rsqrt(variance + EPSILON) * gain_vec

def reference(clip_lengths, inst_frame, query_rows, pix_q, pix_k, pix_v, features, pixel_gain, inst_query, inst_gain):
    spatial = lax.map(spatial_frame, (pix_q, pix_k, pix_v))
    clip_ends = jnp.cumsum(clip_lengths).astype(jnp.int32)
    frame_ids = jnp.arange(FRAMES, dtype=jnp.int32)
    clip_of = lax.optimization_barrier(jnp.sum((clip_ends[None, :] <= frame_ids[:, None]).astype(jnp.int32), axis=1))
    same_clip = clip_of[:, None] == clip_of[None, :]
    time_heads = lax.map(partial(temporal_head, same_clip), (by_heads(pix_q), by_heads(pix_k), by_heads(pix_v)))
    temporal = jnp.moveaxis(time_heads, 0, 1).reshape(FRAMES, C, H, W)
    pixel_pre = features.astype(jnp.float32) + spatial + temporal.astype(jnp.float32)
    pixel_totals = lax.optimization_barrier(jnp.sum(pixel_pre, axis=1, keepdims=True))
    pixel_squares = lax.optimization_barrier(jnp.sum(pixel_pre * pixel_pre, axis=1, keepdims=True))
    pixel_out = normalize(pixel_pre, pixel_totals, pixel_squares, C, pixel_gain[None, :, None, None]).astype(jnp.bfloat16)

    def cross_one(inputs):
        rows_query, frame_num = inputs
        scale_val = HD ** (-0.5)
        key_f = lax.dynamic_index_in_dim(pix_k, frame_num, 0, keepdims=False)
        value_f = lax.dynamic_index_in_dim(pix_v, frame_num, 0, keepdims=False)
        key_h = key_f.astype(jnp.float32).reshape(HEADS, HD, H * W)
        value_h = value_f.astype(jnp.float32).reshape(HEADS, HD, H * W)
        query_h = rows_query.astype(jnp.float32).reshape(QMAX, HEADS, HD)
        scores = jnp.einsum('rnd,ndt->nrt', query_h, key_h) * scale_val
        weights = soft_weights(scores, 2).astype(jnp.float32)
        result = jnp.einsum('nrt,ndt->rnd', weights, value_h)
        return result.reshape(QMAX, C).astype(jnp.bfloat16)
    cross = lax.map(cross_one, (inst_query, inst_frame[:, 0].astype(jnp.int32)))
    inst_pre = inst_query.astype(jnp.float32) + cross.astype(jnp.float32)
    inst_totals = lax.optimization_barrier(jnp.sum(inst_pre, axis=2, keepdims=True))
    inst_squares = lax.optimization_barrier(jnp.sum(inst_pre * inst_pre, axis=2, keepdims=True))
    normed = normalize(inst_pre, inst_totals, inst_squares, C, inst_gain)
    valid = jnp.arange(QMAX, dtype=jnp.int32)[None, :] < query_rows[:, None]
    inst_out = jnp.where(valid[:, :, None], normed, 0.0).astype(jnp.bfloat16)
    return (pixel_out, inst_out)
```

```python
import jax
import jax.numpy as jnp
from jax import lax
from jax.experimental import pallas as pl
from jax.experimental.pallas import tpu as pltpu
from jax.sharding import PartitionSpec as P

F32 = jnp.float32
BF = jnp.bfloat16
MESH = pl.DeviceIdType.MESH
C = 256
HD = 32
EPSILON = 1e-05
MASKED = -1e30
SCALE2 = (HD**-0.5) * 1.4426950408889634
DEAD = 16384.0
CHUNK = 2048
BIG, SMALL = 512, 128
QROWS = 2048 + BIG
VM = pl.BlockSpec(memory_space=pltpu.VMEM)
SM = pl.BlockSpec(memory_space=pltpu.SMEM)


def rows_at(start, size):
    return pl.ds(pl.multiple_of(start, size), size)


def scores_of(k, q):
    return lax.dot_general(k, q, (((0,), (0,)), ((), ())), preferred_element_type=F32)


def width_step(q, k, v):
    s = scores_of(k, q) * SCALE2
    e = jnp.exp2(s - jnp.max(s, axis=0, keepdims=True))
    total = jnp.sum(e, axis=0, keepdims=True)
    return jnp.dot(v, e.astype(BF), preferred_element_type=F32) * (1.0 / total)


def pair_step(q, k, v, low, mask):
    s = scores_of(k, q)
    s = jnp.where(low, s[:64], s[64:]) * SCALE2
    if mask is not None:
        s = s + mask
    e = jnp.exp2(s - jnp.max(s, axis=0, keepdims=True))
    total = jnp.sum(e, axis=0, keepdims=True)
    zero = jnp.zeros_like(e)
    p = jnp.concatenate([jnp.where(low, e, zero), jnp.where(low, zero, e)], axis=0)
    return jnp.dot(v, p.astype(BF), preferred_element_type=F32) * (1.0 / total)


def attend_pairs(qs, ks, vs, os, mask, count, unroll):
    low = lax.broadcasted_iota(jnp.int32, (64, 128), 1) < 64

    def body(b, _):
        r = rows_at(b * 32, 32)
        os[r, :] = pair_step(
            qs[r, :].astype(BF), ks[r, :].astype(BF), vs[r, :].astype(BF), low, mask
        )
        return 0

    lax.fori_loop(0, count, body, 0, unroll=unroll)


def width_all(buf, acc, unroll):
    for f in range(2):

        def body(d, _):
            for half in range(2):
                lanes = pl.ds(half * 128, 128)
                o = width_step(
                    buf[d, pl.ds(f * 32, 32), lanes],
                    buf[d, pl.ds(64 + f * 32, 32), lanes],
                    buf[d, pl.ds(128 + f * 32, 32), lanes],
                )
                acc[pl.ds(f * 2048 + d * 2 + half, 32, stride=64), :] = o
            return 0

        lax.fori_loop(0, 32, body, 0, unroll=unroll)


def height_in(src, dst):
    def body(c, _):
        t = jnp.concatenate([src[0, c], src[1, c]], axis=0).astype(F32)
        dst[pl.ds(c, 128, stride=32), :] = t.T
        return 0

    lax.fori_loop(0, 32, body, 0, unroll=4)


def height_out(os, features, wide, acc):
    def body(c, _):
        t = os[pl.ds(c, 128, stride=32), :].T
        for f in range(2):
            r = rows_at(f * 2048 + c * 64, 64)
            acc[r, :] = wide[r, :] + t[f * 64 : (f + 1) * 64] + features[f, c].astype(F32)
        return 0

    lax.fori_loop(0, 32, body, 0, unroll=4)


BASE = (
    (1, 0), (0, 1), (3, 0), (0, 3), (2, 0), (0, 2), (1, 1), (3, 3),
    (1, 3), (3, 1), (2, 1), (1, 2), (2, 3), (3, 2), (2, 2),
)
MOVES = tuple((a, b, c) for a, b in BASE for c in (0, 1)) + ((0, 0, 1),)


def peer_to(me, move):
    dx, dy, dc = move
    x, y, core = me // 8, (me // 2) % 4, me % 2
    sx = dx + core * ((4 - 2 * dx) % 4)
    sy = dy + core * ((4 - 2 * dy) % 4)
    return ((x + sx) % 4) * 8 + ((y + sy) % 4) * 2 + (core + dc) % 2


def hello(axis, size):
    me = lax.axis_index(axis)
    barrier = pltpu.get_barrier_semaphore()

    def signal(s, _):
        pl.semaphore_signal(
            barrier, inc=1, device_id={axis: lax.rem(me + s, size)}, device_id_type=MESH
        )
        return 0

    lax.fori_loop(1, size, signal, 0)


def greeted(total):
    pl.semaphore_wait(pltpu.get_barrier_semaphore(), total)


def columns_of(row):
    return jnp.broadcast_to(row, (128, 128)).T


def slots_of(trow):
    target = trow.astype(F32)
    one = lax.broadcasted_iota(jnp.int32, (128, 128), 0)
    two = lax.broadcasted_iota(jnp.int32, (128, 128), 1)
    before = jnp.where((columns_of(target) == target) & (one < two), 1.0, 0.0)
    arrival = jnp.sum(before, axis=0, keepdims=True)
    frame = lax.broadcasted_iota(jnp.int32, (64, 128), 0)
    return arrival, jnp.where(frame == trow, 1.0, 0.0).astype(BF)


def first_kernel(
    q, k, v, inst, trow, qrow, buf, kflat, got, stage, rows, msg, raw,
    send_sem, recv_sem, own_sem, load_sem,
):
    me = lax.axis_index("st")
    loads = []
    for number, src in enumerate((k, v, q)):
        load = pltpu.make_async_copy(src, raw.at[number], load_sem.at[number])
        load.start()
        loads.append(load)
    hello("st", 32)
    arrival, place = slots_of(trow[...])
    live = qrow[...].astype(F32)
    group = lax.broadcasted_iota(jnp.int32, (128, 128), 0) // 32
    here = group.astype(F32) == arrival
    counts = lax.dot_general(
        place,
        jnp.where(here, live, 0.0).astype(BF),
        (((1,), (1,)), ((), ())),
        preferred_element_type=F32,
    )
    for r in range(16):
        x = inst[r].astype(F32)
        y = jnp.where(here, jnp.concatenate([x, x, x, x], axis=0), 0.0).astype(BF)
        put = lax.dot_general(
            place, y, (((1,), (1,)), ((), ())), preferred_element_type=F32
        )
        rows[pl.ds(r, 64, stride=16), :] = jnp.where(counts > r + 0.5, put, DEAD)
    msg[...] = rows[...].astype(BF)
    greeted(31)
    copies = []
    for i, move in enumerate(MOVES):
        peer = peer_to(me, move)
        copy = pltpu.make_async_remote_copy(
            src_ref=msg.at[rows_at(peer * 32, 32)],
            dst_ref=got.at[rows_at(me * 32, 32)],
            send_sem=send_sem.at[i],
            recv_sem=recv_sem.at[i],
            device_id={"st": peer},
            device_id_type=MESH,
        )
        copy.start()
        copies.append(copy)
    own = pltpu.make_async_copy(
        msg.at[rows_at(me * 32, 32)], got.at[rows_at(me * 32, 32)], own_sem
    )
    own.start()
    for number in range(3):
        base = (64, 128, 0)[number]
        loads[number].wait()

        def widen(c, _):
            for f in range(2):
                stage[rows_at(f * 2048 + c * 64, 64), :] = raw[number, f, c].astype(F32)
            return 0

        lax.fori_loop(0, 32, widen, 0, unroll=4)

        def body(d, _):
            for half in range(2):
                x = stage[pl.ds(d * 2 + half, 64, stride=64), :].astype(BF)
                buf[d, pl.ds(base, 64), pl.ds(half * 128, 128)] = x
                if number == 0:
                    kflat[:, rows_at((d * 2 + half) * 128, 128)] = x
            return 0

        lax.fori_loop(0, 32, body, 0, unroll=4)
    own.wait()
    for copy in copies:
        copy.wait()


def first(q, k, v, inst, trow, qrow):
    sd = jax.ShapeDtypeStruct
    dma = pltpu.SemaphoreType.DMA
    any_space = pl.BlockSpec(memory_space=pl.ANY)
    return pl.pallas_call(
        first_kernel,
        out_shape=(sd((32, 192, 256), BF), sd((64, 8192), BF), sd((1024, 128), BF)),
        in_specs=[any_space] * 3 + [VM] * 3,
        out_specs=(VM, VM, VM),
        scratch_shapes=[
            pltpu.VMEM((4096, 128), F32),
            pltpu.VMEM((1024, 128), F32),
            pltpu.VMEM((1024, 128), BF),
            pltpu.VMEM((3, 2, 32, 64, 128), BF),
            dma((31,)),
            dma((31,)),
            dma,
            dma((3,)),
        ],
        compiler_params=pltpu.CompilerParams(
            collective_id=0, has_side_effects=True, vmem_limit_bytes=20 << 20
        ),
        cost_estimate=pl.CostEstimate(flops=1 << 24, bytes_accessed=8 << 20, transcendentals=0),
    )(q, k, v, inst, trow, qrow)


def cross_block(q, kflat, values, f):
    most, acc = None, None
    for j in range(8192 // CHUNK):
        s = jnp.dot(
            q,
            kflat[f * 32 : (f + 1) * 32, j * CHUNK : (j + 1) * CHUNK],
            preferred_element_type=F32,
        )
        here = jnp.max(s, axis=1, keepdims=True) * SCALE2
        new = here if most is None else jnp.maximum(most, here)
        p = jnp.exp2(s * SCALE2 - new).astype(BF)
        o = jnp.dot(p, values[f, pl.ds(j * CHUNK, CHUNK), :], preferred_element_type=F32)
        acc = o if acc is None else acc * jnp.exp2(most - new) + o
        most = new
    return acc / acc[:, 32:33]


def cross_kernel(got, kflat, buf, ans, acc, values, wide, packed, solved, live, counts, starts, sem):
    wide[...] = got[...].astype(F32)
    alive = jnp.where(wide[...] < DEAD / 2, 1.0, 0.0).reshape(64, 16, 128)
    live[...] = jnp.sum(alive, axis=1).astype(jnp.int32)
    down = pltpu.make_async_copy(live, counts, sem)
    down.start()

    def turn(d, _):
        for f in range(2):
            t = buf[d, pl.ds(128 + f * 32, 32), :].astype(F32)
            one = jnp.ones((32, 256), F32)
            full = jnp.concatenate([t, one, one, one], axis=0)
            values[f, rows_at(d * 256, 256), :] = full.T.astype(BF)
        return 0

    lax.fori_loop(0, 32, turn, 0, unroll=2)
    down.wait()
    width_all(buf, acc, 8)

    for f in range(2):

        def pack(src, offset):
            block = wide[pl.ds(pl.multiple_of(src * 32 + f * 16, 16), 16), :]
            for j in range(4):
                starts[src * 2 + f, j] = offset
                moved = block if j == 0 else pltpu.roll(block, 128 - 32 * j, 1)
                packed[pl.ds(offset, 16), :] = moved
                offset = offset + counts[src * 2 + f, 32 * j]
            return offset

        total = lax.fori_loop(0, 32, pack, 0)
        many = (total + SMALL - 1) // BIG
        rest = jnp.maximum(total - many * BIG, 0)

        def big(b, _):
            r = rows_at(b * BIG, BIG)
            solved[r, :] = cross_block(packed[r, :][:, :32].astype(BF), kflat, values, f)
            return 0

        lax.fori_loop(0, many, big, 0)

        def small(b, _):
            r = rows_at(many * BIG + b * SMALL, SMALL)
            solved[r, :] = cross_block(packed[r, :][:, :32].astype(BF), kflat, values, f)
            return 0

        lax.fori_loop(0, (rest + SMALL - 1) // SMALL, small, 0)
        row = lax.broadcasted_iota(jnp.int32, (16, 128), 0)
        group = lax.broadcasted_iota(jnp.int32, (16, 128), 1) // 32

        def unpack(src, _):
            out = jnp.zeros((16, 128), F32)
            for j in range(4):
                x = solved[pl.ds(starts[src * 2 + f, j], 16), :]
                moved = x if j == 0 else pltpu.roll(x, 32 * j, 1)
                keep = (group == j) & (row < counts[src * 2 + f, 32 * j])
                out = jnp.where(keep, moved, out)
            ans[pl.ds(pl.multiple_of(src * 32 + f * 16, 16), 16), :] = out.astype(BF)
            return 0

        lax.fori_loop(0, 32, unpack, 0)


def cross(got, kflat, buf):
    return pl.pallas_call(
        cross_kernel,
        out_shape=(
            jax.ShapeDtypeStruct((1024, 128), BF),
            jax.ShapeDtypeStruct((4096, 128), F32),
        ),
        in_specs=[VM] * 3,
        out_specs=(VM, VM),
        scratch_shapes=[
            pltpu.VMEM((2, 8192, 128), BF),
            pltpu.VMEM((1024, 128), F32),
            pltpu.VMEM((QROWS, 128), F32),
            pltpu.VMEM((QROWS, 128), F32),
            pltpu.VMEM((64, 128), jnp.int32),
            pltpu.SMEM((64, 128), jnp.int32),
            pltpu.SMEM((64, 4), jnp.int32),
            pltpu.SemaphoreType.DMA,
        ],
        compiler_params=pltpu.CompilerParams(vmem_limit_bytes=32 << 20),
        cost_estimate=pl.CostEstimate(
            flops=17 << 30, bytes_accessed=8 << 20, transcendentals=1 << 24
        ),
    )(got, kflat, buf)


def time_half(patch, mask, half, stage, qs, ks, vs, os, out):
    low = lax.broadcasted_iota(jnp.int32, (64, 128), 1) < 64
    lanes = pl.ds(half * 128, 128)
    for base, dst in ((0, qs), (64, ks), (128, vs)):

        def spread(i, _):
            stage[rows_at(i * 64, 64), :] = patch[i, pl.ds(base, 64), lanes].astype(F32)
            return 0

        lax.fori_loop(0, 32, spread, 0, unroll=4)

        def turn(b, _):
            one, two = pl.ds(b * 2, 64, stride=32), pl.ds(b * 2 + 1, 64, stride=32)
            t = jnp.concatenate([stage[one, :], stage[two, :]], axis=0).T
            top, end = t[:64], t[64:]
            dst[one, :] = jnp.where(low, top, pltpu.roll(end, 64, 1))
            dst[two, :] = jnp.where(low, pltpu.roll(top, 64, 1), end)
            return 0

        lax.fori_loop(0, 16, turn, 0, unroll=4)
    attend_pairs(qs, ks, vs, os, mask, 64, 16)

    def turn_back(b, _):
        one, two = pl.ds(b * 2, 64, stride=32), pl.ds(b * 2 + 1, 64, stride=32)
        x, y = os[one, :], os[two, :]
        top = jnp.where(low, x, pltpu.roll(y, 64, 1))
        end = jnp.where(low, pltpu.roll(x, 64, 1), y)
        t = jnp.concatenate([top, end], axis=0).T
        stage[one, :] = t[:64]
        stage[two, :] = t[64:]
        return 0

    lax.fori_loop(0, 16, turn_back, 0, unroll=4)

    def gather(i, _):
        out[half, i] = stage[rows_at(i * 64, 64), :].astype(BF)
        return 0

    lax.fori_loop(0, 32, gather, 0, unroll=4)


def last_kernel(
    patch, mask, ans, q, k, v, features, wide, inst, trow,
    acc, pall, irow, istat,
    raw, timed, tback, aback, stage, qs, ks, vs, os, arow, part, partbf, pgot, pnew,
    ipart, igot, tsend, trecv, asend, arecv, own_sem, zsend, zrecv, load_sem,
):
    me = lax.axis_index("st")
    mz = lax.axis_index("ha")
    hello("st", 32)
    hello("ha", 8)
    loads = []
    for number, src in enumerate((q, k, v, features)):
        load = pltpu.make_async_copy(src, raw.at[number], load_sem.at[number])
        load.start()
        loads.append(load)

    def to_st(src, dst, send, recv, i, peer):
        copy = pltpu.make_async_remote_copy(
            src_ref=src,
            dst_ref=dst,
            send_sem=send.at[i],
            recv_sem=recv.at[i],
            device_id={"st": peer},
            device_id_type=MESH,
        )
        copy.start()
        return copy

    def return_half(half):
        copies = [
            to_st(
                timed.at[half, peer_to(me, move)], tback.at[half, me],
                tsend.at[half], trecv.at[half], i, peer_to(me, move),
            )
            for i, move in enumerate(MOVES)
        ]
        own = pltpu.make_async_copy(
            timed.at[half, me], tback.at[half, me], own_sem.at[half]
        )
        own.start()
        return copies + [own]

    known = mask[...]
    time_half(patch, known, 0, stage, qs, ks, vs, os, timed)
    greeted(38)
    answers = []
    for i, move in enumerate(MOVES):
        peer = peer_to(me, move)
        answers.append(
            to_st(
                ans.at[rows_at(peer * 32, 32)], aback.at[rows_at(me * 32, 32)],
                asend, arecv, i, peer,
            )
        )
    own = pltpu.make_async_copy(
        ans.at[rows_at(me * 32, 32)], aback.at[rows_at(me * 32, 32)], own_sem.at[2]
    )
    own.start()
    answers.append(own)
    backs = return_half(0)
    time_half(patch, known, 1, stage, qs, ks, vs, os, timed)
    backs = backs + return_half(1)

    for load in loads:
        load.wait()
    height_in(raw.at[0], qs)
    height_in(raw.at[1], ks)
    height_in(raw.at[2], vs)
    attend_pairs(qs, ks, vs, os, None, 128, 16)
    height_out(os, raw.at[3], wide, acc)

    def exchange(src, dst, at_src, at_dst, which):
        copies = []
        for s in range(1, 8):
            peer = lax.rem(mz + s, 8)
            copy = pltpu.make_async_remote_copy(
                src_ref=at_src(src, peer),
                dst_ref=at_dst(dst),
                send_sem=zsend.at[which, s],
                recv_sem=zrecv.at[which, s],
                device_id={"ha": peer},
                device_id_type=MESH,
            )
            copy.start()
            copies.append(copy)
        return copies

    arrival, place = slots_of(trow[...])
    for copy in answers:
        copy.wait()
    arow[...] = aback[...].astype(F32)
    for r in range(16):
        mine = lax.dot_general(
            arow[pl.ds(r, 64, stride=16), :].astype(BF),
            place,
            (((0,), (0,)), ((), ())),
            preferred_element_type=F32,
        )
        pre = inst[r].astype(F32)
        for j in range(4):
            pre = pre + jnp.where(arrival == j, mine[j * 32 : (j + 1) * 32], 0.0)
        irow[r] = pre
        ipart[pl.ds(r, 1), :] = jnp.sum(pre, axis=0, keepdims=True)
        ipart[pl.ds(16 + r, 1), :] = jnp.sum(pre * pre, axis=0, keepdims=True)
    shared = exchange(ipart, igot, lambda a, p: a, lambda a: a.at[mz], 0)
    igot[mz] = ipart[...]

    for copy in backs:
        copy.wait()

    def add_time(d, _):
        for half in range(2):
            r = pl.ds(d * 2 + half, 64, stride=64)
            acc[r, :] = acc[r, :] + tback[half, d].astype(F32)
        return 0

    lax.fori_loop(0, 32, add_time, 0, unroll=4)
    for f in range(2):

        def sums(c, carry):
            x = acc[rows_at(f * 2048 + c * 64, 64), :]
            return carry[0] + x, carry[1] + x * x

        zero = jnp.zeros((64, 128), F32)
        tot, sqr = lax.fori_loop(0, 32, sums, (zero, zero), unroll=4)
        for b in range(4):
            part[f * 4 + b, 0:16, :] = tot[b * 16 : (b + 1) * 16]
            part[f * 4 + b, 16:32, :] = sqr[b * 16 : (b + 1) * 16]
    partbf[...] = part[...].astype(BF)
    scattered = exchange(partbf, pgot, lambda a, p: a.at[p], lambda a: a.at[mz], 1)
    pgot[mz] = partbf[mz]
    for copy in shared:
        copy.wait()
    total = igot[0]
    for z in range(1, 8):
        total = total + igot[z]
    mean = total[:16] / C
    istat[0:16, :] = mean
    istat[16:32, :] = lax.rsqrt(total[16:] / C - mean * mean + EPSILON)
    for copy in scattered:
        copy.wait()
    total = pgot[0].astype(F32)
    for z in range(1, 8):
        total = total + pgot[z].astype(F32)
    mean = total[:16] / C
    pnew[0:16, :] = mean
    pnew[16:32, :] = lax.rsqrt(total[16:] / C - mean * mean + EPSILON)
    gathered = exchange(pnew, pall, lambda a, p: a, lambda a: a.at[mz], 2)
    pall[mz] = pnew[...]
    for copy in gathered:
        copy.wait()


def last(patch, mask, ans, q, k, v, features, wide, inst, trow):
    sd = jax.ShapeDtypeStruct
    dma = pltpu.SemaphoreType.DMA
    any_space = pl.BlockSpec(memory_space=pl.ANY)
    return pl.pallas_call(
        last_kernel,
        out_shape=(
            sd((4096, 128), F32),
            sd((8, 32, 128), F32),
            sd((16, 32, 128), F32),
            sd((32, 128), F32),
        ),
        in_specs=[VM] * 3 + [any_space] * 4 + [VM] * 3,
        out_specs=(VM, VM, VM, VM),
        scratch_shapes=[
            pltpu.VMEM((4, 2, 32, 64, 128), BF),
            pltpu.VMEM((2, 32, 64, 128), BF),
            pltpu.VMEM((2, 32, 64, 128), BF),
            pltpu.VMEM((1024, 128), BF),
            pltpu.VMEM((2048, 128), F32),
            pltpu.VMEM((4096, 128), F32),
            pltpu.VMEM((4096, 128), F32),
            pltpu.VMEM((4096, 128), F32),
            pltpu.VMEM((4096, 128), F32),
            pltpu.VMEM((1024, 128), F32),
            pltpu.VMEM((8, 32, 128), F32),
            pltpu.VMEM((8, 32, 128), BF),
            pltpu.VMEM((8, 32, 128), BF),
            pltpu.VMEM((32, 128), F32),
            pltpu.VMEM((32, 128), F32),
            pltpu.VMEM((8, 32, 128), F32),
            dma((2, 31)),
            dma((2, 31)),
            dma((31,)),
            dma((31,)),
            dma((3,)),
            dma((3, 8)),
            dma((3, 8)),
            dma((4,)),
        ],
        compiler_params=pltpu.CompilerParams(
            collective_id=1, has_side_effects=True, vmem_limit_bytes=34 << 20
        ),
        cost_estimate=pl.CostEstimate(
            flops=1 << 32, bytes_accessed=12 << 20, transcendentals=1 << 21
        ),
    )(patch, mask, ans, q, k, v, features, wide, inst, trow)


def norm_kernel(acc, pall, irow, istat, qrow, pgain, igain, pixel_out, inst_out):
    for f in range(2):

        def finish(c, _):
            r = rows_at(f * 2048 + c * 64, 64)
            gain = pgain[c]
            x = acc[r, :]
            for b in range(4):
                low = slice(b * 16, (b + 1) * 16)
                y = (x[low] - pall[f * 4 + b, 0:16, :]) * pall[f * 4 + b, 16:32, :] * gain
                pixel_out[f, c, low, :] = y.astype(BF)
            return 0

        lax.fori_loop(0, 32, finish, 0, unroll=4)
    row = igain[...]
    gains = columns_of(jnp.concatenate([row, row, row, row], axis=1))[:32]
    live = qrow[...]
    for r in range(16):
        y = (irow[r] - istat[pl.ds(r, 1), :]) * istat[pl.ds(16 + r, 1), :] * gains
        inst_out[r] = jnp.where(live > r, y, 0.0).astype(BF)


def norm(acc, pall, irow, istat, qrow, pgain, igain):
    sd = jax.ShapeDtypeStruct
    return pl.pallas_call(
        norm_kernel,
        out_shape=(sd((2, 32, 64, 128), BF), sd((16, 32, 128), BF)),
        in_specs=[VM] * 5 + [SM, VM],
        out_specs=(VM, VM),
        compiler_params=pltpu.CompilerParams(vmem_limit_bytes=12 << 20),
        cost_estimate=pl.CostEstimate(flops=1 << 22, bytes_accessed=3 << 20, transcendentals=0),
    )(acc, pall, irow, istat, qrow, pgain, igain)


def per_device(
    clip_lengths,
    inst_frame,
    query_rows,
    pix_q,
    pix_k,
    pix_v,
    features,
    pixel_gain,
    inst_query,
    inst_gain,
):
    clip_ends = jnp.cumsum(clip_lengths)
    frame_ids = jnp.arange(64, dtype=jnp.int32)
    clip_of = jnp.sum((clip_ends[None, :] <= frame_ids[:, None]).astype(jnp.int32), axis=1)
    same_clip = clip_of[:, None] == clip_of[None, :]
    mask = jnp.where(same_clip, 0.0, MASKED).astype(F32)
    mask = jnp.concatenate([mask, mask], axis=1)
    trow = inst_frame.reshape(1, 128)
    qrow = query_rows.reshape(1, 128)
    inst = inst_query.transpose(1, 2, 0)
    buf, kflat, got = first(pix_q, pix_k, pix_v, inst, trow, qrow)
    buf, got = lax.optimization_barrier((buf, got))
    patch = lax.all_to_all(buf, "st", split_axis=0, concat_axis=0, tiled=True)
    ans, wide = cross(got, kflat, buf)
    acc, pall, irow, istat = last(
        patch, mask, ans, pix_q, pix_k, pix_v, features, wide, inst, trow
    )
    pixel_out, inst_out = norm(
        acc, pall, irow, istat, qrow, pixel_gain, inst_gain.reshape(1, 32)
    )
    return pixel_out, inst_out.transpose(2, 0, 1)


def solution(mesh):
    placed = (
        P(),
        P("st", None),
        P("st"),
        P("st", "ha", None, None),
        P("st", "ha", None, None),
        P("st", "ha", None, None),
        P("st", "ha", None, None),
        P("ha"),
        P("st", None, "ha"),
        P("ha"),
    )
    return jax.shard_map(
        per_device,
        mesh=mesh,
        in_specs=placed,
        out_specs=(P("st", "ha", None, None), P("st", None, "ha")),
        check_vma=False,
    )
```

```python
import jax
import jax.numpy as jnp
from jax import lax
from jax.experimental import pallas as pl
from jax.experimental.pallas import tpu as pltpu
from jax.sharding import PartitionSpec as P

F32 = jnp.float32
BF = jnp.bfloat16
MESH = pl.DeviceIdType.MESH
C = 256
HD = 32
EPSILON = 1e-05
MASKED = -1e30
SCALE2 = (HD**-0.5) * 1.4426950408889634
DEAD = 16384.0
CHUNK = 2048
BIG, SMALL = 512, 128
QROWS = 2048 + BIG
VM = pl.BlockSpec(memory_space=pltpu.VMEM)
SM = pl.BlockSpec(memory_space=pltpu.SMEM)
HB = pl.BlockSpec(memory_space=pltpu.HBM)


def rows_at(start, size):
    return pl.ds(pl.multiple_of(start, size), size)


def scores_of(k, q):
    return lax.dot_general(k, q, (((0,), (0,)), ((), ())), preferred_element_type=F32)


def width_step(q, k, v):
    s = scores_of(k, q) * SCALE2
    e = jnp.exp2(s - jnp.max(s, axis=0, keepdims=True))
    total = jnp.sum(e, axis=0, keepdims=True)
    return jnp.dot(v, e.astype(BF), preferred_element_type=F32) * (1.0 / total)


def pair_step(q, k, v, low, mask):
    s = scores_of(k, q)
    s = jnp.where(low, s[:64], s[64:]) * SCALE2
    if mask is not None:
        s = s + mask
    e = jnp.exp2(s - jnp.max(s, axis=0, keepdims=True))
    total = jnp.sum(e, axis=0, keepdims=True)
    zero = jnp.zeros_like(e)
    p = jnp.concatenate([jnp.where(low, e, zero), jnp.where(low, zero, e)], axis=0)
    return jnp.dot(v, p.astype(BF), preferred_element_type=F32) * (1.0 / total)


def attend_pairs(qs, ks, vs, os, mask, count, unroll):
    low = lax.broadcasted_iota(jnp.int32, (64, 128), 1) < 64

    def body(b, _):
        r = rows_at(b * 32, 32)
        os[r, :] = pair_step(
            qs[r, :].astype(BF), ks[r, :].astype(BF), vs[r, :].astype(BF), low, mask
        )
        return 0

    lax.fori_loop(0, count, body, 0, unroll=unroll)


def width_all(buf, acc, unroll):
    for f in range(2):

        def body(d, _):
            for half in range(2):
                lanes = pl.ds(half * 128, 128)
                o = width_step(
                    buf[d, pl.ds(f * 32, 32), lanes],
                    buf[d, pl.ds(64 + f * 32, 32), lanes],
                    buf[d, pl.ds(128 + f * 32, 32), lanes],
                )
                r = pl.ds(f * 2048 + d * 2 + half, 32, stride=64)
                acc[r, :] = acc[r, :] + o
            return 0

        lax.fori_loop(0, 32, body, 0, unroll=unroll)


def height_in(src, dst):
    def body(c, _):
        t = jnp.concatenate([src[0, c], src[1, c]], axis=0).astype(F32)
        dst[pl.ds(c, 128, stride=32), :] = t.T
        return 0

    lax.fori_loop(0, 32, body, 0, unroll=4)


def height_out(os, features, acc):
    def body(c, _):
        t = os[pl.ds(c, 128, stride=32), :].T
        for f in range(2):
            r = rows_at(f * 2048 + c * 64, 64)
            acc[r, :] = t[f * 64 : (f + 1) * 64] + features[f, c].astype(F32)
        return 0

    lax.fori_loop(0, 32, body, 0, unroll=4)


BASE = (
    (1, 0), (0, 1), (3, 0), (0, 3), (2, 0), (0, 2), (1, 1), (3, 3),
    (1, 3), (3, 1), (2, 1), (1, 2), (2, 3), (3, 2), (2, 2),
)
MOVES = tuple((a, b, c) for a, b in BASE for c in (0, 1)) + ((0, 0, 1),)


def peer_to(me, move):
    dx, dy, dc = move
    x, y, core = me // 8, (me // 2) % 4, me % 2
    sx = dx + core * ((4 - 2 * dx) % 4)
    sy = dy + core * ((4 - 2 * dy) % 4)
    return ((x + sx) % 4) * 8 + ((y + sy) % 4) * 2 + (core + dc) % 2


def hello(axis, size):
    me = lax.axis_index(axis)
    barrier = pltpu.get_barrier_semaphore()

    def signal(s, _):
        pl.semaphore_signal(
            barrier, inc=1, device_id={axis: lax.rem(me + s, size)}, device_id_type=MESH
        )
        return 0

    lax.fori_loop(1, size, signal, 0)


def greeted(total):
    pl.semaphore_wait(pltpu.get_barrier_semaphore(), total)


def columns_of(row):
    return jnp.broadcast_to(row, (128, 128)).T


def slots_of(trow):
    target = trow.astype(F32)
    one = lax.broadcasted_iota(jnp.int32, (128, 128), 0)
    two = lax.broadcasted_iota(jnp.int32, (128, 128), 1)
    before = jnp.where((columns_of(target) == target) & (one < two), 1.0, 0.0)
    arrival = jnp.sum(before, axis=0, keepdims=True)
    frame = lax.broadcasted_iota(jnp.int32, (64, 128), 0)
    return arrival, jnp.where(frame == trow, 1.0, 0.0).astype(BF)


def first_kernel(
    q, k, v, inst_hbm, trow, qrow, buf_hbm, kflat_hbm, got,
    stage, rows, msg, raw, inst, buf, kflat,
    send_sem, recv_sem, own_sem, load_sem, save_sem,
):
    me = lax.axis_index("st")
    load_inst = pltpu.make_async_copy(inst_hbm, inst, load_sem.at[3])
    load_inst.start()
    loads = []
    for number, src in enumerate((k, v, q)):
        load = pltpu.make_async_copy(src, raw.at[number], load_sem.at[number])
        load.start()
        loads.append(load)
    hello("st", 32)
    arrival, place = slots_of(trow[...])
    live = qrow[...].astype(F32)
    group = lax.broadcasted_iota(jnp.int32, (128, 128), 0) // 32
    here = group.astype(F32) == arrival
    counts = lax.dot_general(
        place,
        jnp.where(here, live, 0.0).astype(BF),
        (((1,), (1,)), ((), ())),
        preferred_element_type=F32,
    )
    load_inst.wait()
    for r in range(16):
        x = inst[r].astype(F32)
        y = jnp.where(here, jnp.concatenate([x, x, x, x], axis=0), 0.0).astype(BF)
        put = lax.dot_general(
            place, y, (((1,), (1,)), ((), ())), preferred_element_type=F32
        )
        rows[pl.ds(r, 64, stride=16), :] = jnp.where(counts > r + 0.5, put, DEAD)
    msg[...] = rows[...].astype(BF)
    greeted(31)
    copies = []
    for i, move in enumerate(MOVES):
        peer = peer_to(me, move)
        copy = pltpu.make_async_remote_copy(
            src_ref=msg.at[rows_at(peer * 32, 32)],
            dst_ref=got.at[rows_at(me * 32, 32)],
            send_sem=send_sem.at[i],
            recv_sem=recv_sem.at[i],
            device_id={"st": peer},
            device_id_type=MESH,
        )
        copy.start()
        copies.append(copy)
    own = pltpu.make_async_copy(
        msg.at[rows_at(me * 32, 32)], got.at[rows_at(me * 32, 32)], own_sem
    )
    own.start()
    saves = []
    for number in range(3):
        base = (64, 128, 0)[number]
        loads[number].wait()

        def widen(c, _):
            for f in range(2):
                stage[rows_at(f * 2048 + c * 64, 64), :] = raw[number, f, c].astype(F32)
            return 0

        lax.fori_loop(0, 32, widen, 0, unroll=4)

        def body(d, _):
            for half in range(2):
                x = stage[pl.ds(d * 2 + half, 64, stride=64), :].astype(BF)
                buf[d, pl.ds(base, 64), pl.ds(half * 128, 128)] = x
                if number == 0:
                    kflat[:, rows_at((d * 2 + half) * 128, 128)] = x
            return 0

        lax.fori_loop(0, 32, body, 0, unroll=4)
        part = pl.ds(base, 64)
        save = pltpu.make_async_copy(
            buf.at[:, part, :], buf_hbm.at[:, part, :], save_sem.at[number]
        )
        save.start()
        saves.append(save)
        if number == 0:
            save = pltpu.make_async_copy(kflat, kflat_hbm, save_sem.at[3])
            save.start()
            saves.append(save)
    for save in saves:
        save.wait()
    own.wait()
    for copy in copies:
        copy.wait()


def first(q, k, v, inst, trow, qrow):
    sd = jax.ShapeDtypeStruct
    dma = pltpu.SemaphoreType.DMA
    return pl.pallas_call(
        first_kernel,
        out_shape=(sd((32, 192, 256), BF), sd((64, 8192), BF), sd((1024, 128), BF)),
        in_specs=[HB] * 4 + [VM] * 2,
        out_specs=(HB, HB, HB),
        scratch_shapes=[
            pltpu.VMEM((4096, 128), F32),
            pltpu.VMEM((1024, 128), F32),
            pltpu.VMEM((1024, 128), BF),
            pltpu.VMEM((3, 2, 32, 64, 128), BF),
            pltpu.VMEM((16, 32, 128), BF),
            pltpu.VMEM((32, 192, 256), BF),
            pltpu.VMEM((64, 8192), BF),
            dma((31,)),
            dma((31,)),
            dma,
            dma((4,)),
            dma((4,)),
        ],
        compiler_params=pltpu.CompilerParams(
            collective_id=0, has_side_effects=True, vmem_limit_bytes=60 << 20
        ),
        cost_estimate=pl.CostEstimate(flops=1 << 24, bytes_accessed=8 << 20, transcendentals=0),
    )(q, k, v, inst, trow, qrow)


def cross_block(q, kflat, values, f):
    most, acc = None, None
    for j in range(8192 // CHUNK):
        s = jnp.dot(
            q,
            kflat[f * 32 : (f + 1) * 32, j * CHUNK : (j + 1) * CHUNK],
            preferred_element_type=F32,
        )
        here = jnp.max(s, axis=1, keepdims=True) * SCALE2
        new = here if most is None else jnp.maximum(most, here)
        p = jnp.exp2(s * SCALE2 - new).astype(BF)
        o = jnp.dot(p, values[pl.ds(j * CHUNK, CHUNK), :], preferred_element_type=F32)
        acc = o if acc is None else acc * jnp.exp2(most - new) + o
        most = new
    return acc / acc[:, 64:65]


def middle_kernel(
    got_hbm, kflat_hbm, buf_hbm, q, k, v, features, ans_hbm, wide_hbm,
    got, kflat, buf, raw, ans, acc, qs, ks, vs, os,
    values, wide, packed, solved, live, counts, starts, sem,
):
    pairs = ((got_hbm, got), (buf_hbm, buf)) + tuple(
        (src, raw.at[i]) for i, src in enumerate((q, k, v, features))
    ) + ((kflat_hbm, kflat),)
    loads = [pltpu.make_async_copy(x, y, sem.at[i]) for i, (x, y) in enumerate(pairs)]
    for load in loads:
        load.start()
    loads[0].wait()
    wide[...] = got[...].astype(F32)
    alive = jnp.where(wide[...] < DEAD / 2, 1.0, 0.0).reshape(64, 16, 128)
    live[...] = jnp.sum(alive, axis=1).astype(jnp.int32)
    down = pltpu.make_async_copy(live, counts, sem.at[7])
    down.start()
    loads[1].wait()

    def turn(d, _):
        t = buf[d, pl.ds(128, 64), :].astype(F32)
        full = jnp.concatenate([t, jnp.ones((64, 256), F32)], axis=0)
        values[rows_at(d * 256, 256), :] = full.T.astype(BF)
        return 0

    lax.fori_loop(0, 32, turn, 0, unroll=2)
    for load in loads[2:]:
        load.wait()
    height_in(raw.at[0], qs)
    height_in(raw.at[1], ks)
    height_in(raw.at[2], vs)
    attend_pairs(qs, ks, vs, os, None, 128, 32)
    height_out(os, raw.at[3], acc)
    save = pltpu.make_async_copy(acc, wide_hbm, sem.at[8])
    save.start()
    down.wait()

    for f in range(2):

        def pack(src, offset):
            block = wide[pl.ds(pl.multiple_of(src * 32 + f * 16, 16), 16), :]
            for j in range(4):
                starts[src * 2 + f, j] = offset
                moved = block if j == 0 else pltpu.roll(block, 128 - 32 * j, 1)
                packed[pl.ds(offset, 16), :] = moved
                offset = offset + counts[src * 2 + f, 32 * j]
            return offset

        total = lax.fori_loop(0, 32, pack, 0, unroll=4)
        many = (total + SMALL - 1) // BIG
        rest = jnp.maximum(total - many * BIG, 0)

        def big(b, _):
            r = rows_at(b * BIG, BIG)
            solved[r, :] = cross_block(packed[r, :][:, :32].astype(BF), kflat, values, f)
            return 0

        lax.fori_loop(0, many, big, 0)

        def small(b, _):
            r = rows_at(many * BIG + b * SMALL, SMALL)
            solved[r, :] = cross_block(packed[r, :][:, :32].astype(BF), kflat, values, f)
            return 0

        lax.fori_loop(0, (rest + SMALL - 1) // SMALL, small, 0)
        row = lax.broadcasted_iota(jnp.int32, (16, 128), 0)
        group = lax.broadcasted_iota(jnp.int32, (16, 128), 1) // 32

        def unpack(src, _):
            out = jnp.zeros((16, 128), F32)
            for j in range(4):
                x = solved[pl.ds(starts[src * 2 + f, j], 16), :]
                shift = (32 * (j - f)) % 128
                moved = x if shift == 0 else pltpu.roll(x, shift, 1)
                keep = (group == j) & (row < counts[src * 2 + f, 32 * j])
                out = jnp.where(keep, moved, out)
            ans[pl.ds(pl.multiple_of(src * 32 + f * 16, 16), 16), :] = out.astype(BF)
            return 0

        lax.fori_loop(0, 32, unpack, 0, unroll=4)
    back = pltpu.make_async_copy(ans, ans_hbm, sem.at[9])
    back.start()
    back.wait()
    save.wait()


def middle(got, kflat, buf, q, k, v, features):
    sd = jax.ShapeDtypeStruct
    return pl.pallas_call(
        middle_kernel,
        out_shape=(sd((1024, 128), BF), sd((4096, 128), F32)),
        in_specs=[HB] * 7,
        out_specs=(HB, HB),
        scratch_shapes=[
            pltpu.VMEM((1024, 128), BF),
            pltpu.VMEM((64, 8192), BF),
            pltpu.VMEM((32, 192, 256), BF),
            pltpu.VMEM((4, 2, 32, 64, 128), BF),
            pltpu.VMEM((1024, 128), BF),
            pltpu.VMEM((4096, 128), F32),
            pltpu.VMEM((4096, 128), F32),
            pltpu.VMEM((4096, 128), F32),
            pltpu.VMEM((4096, 128), F32),
            pltpu.VMEM((4096, 128), F32),
            pltpu.VMEM((8192, 128), BF),
            pltpu.VMEM((1024, 128), F32),
            pltpu.VMEM((QROWS, 128), F32),
            pltpu.VMEM((QROWS, 128), F32),
            pltpu.VMEM((64, 128), jnp.int32),
            pltpu.SMEM((64, 128), jnp.int32),
            pltpu.SMEM((64, 4), jnp.int32),
            pltpu.SemaphoreType.DMA((10,)),
        ],
        compiler_params=pltpu.CompilerParams(vmem_limit_bytes=60 << 20),
        cost_estimate=pl.CostEstimate(
            flops=17 << 30, bytes_accessed=8 << 20, transcendentals=1 << 24
        ),
    )(got, kflat, buf, q, k, v, features)


def time_half(patch, mask, half, stage, qs, ks, vs, os, out):
    low = lax.broadcasted_iota(jnp.int32, (64, 128), 1) < 64
    lanes = pl.ds(half * 128, 128)
    for base, dst in ((0, qs), (64, ks), (128, vs)):

        def spread(i, _):
            stage[rows_at(i * 64, 64), :] = patch[i, pl.ds(base, 64), lanes].astype(F32)
            return 0

        lax.fori_loop(0, 32, spread, 0, unroll=4)

        def turn(b, _):
            one, two = pl.ds(b * 2, 64, stride=32), pl.ds(b * 2 + 1, 64, stride=32)
            t = jnp.concatenate([stage[one, :], stage[two, :]], axis=0).T
            top, end = t[:64], t[64:]
            dst[one, :] = jnp.where(low, top, pltpu.roll(end, 64, 1))
            dst[two, :] = jnp.where(low, pltpu.roll(top, 64, 1), end)
            return 0

        lax.fori_loop(0, 16, turn, 0, unroll=4)
    attend_pairs(qs, ks, vs, os, mask, 64, 32)

    def turn_back(b, _):
        one, two = pl.ds(b * 2, 64, stride=32), pl.ds(b * 2 + 1, 64, stride=32)
        x, y = os[one, :], os[two, :]
        top = jnp.where(low, x, pltpu.roll(y, 64, 1))
        end = jnp.where(low, pltpu.roll(x, 64, 1), y)
        t = jnp.concatenate([top, end], axis=0).T
        stage[one, :] = t[:64]
        stage[two, :] = t[64:]
        return 0

    lax.fori_loop(0, 16, turn_back, 0, unroll=4)

    def gather(i, _):
        out[half, i] = stage[rows_at(i * 64, 64), :].astype(BF)
        return 0

    lax.fori_loop(0, 32, gather, 0, unroll=4)


def last_kernel(
    patch, mask, ans, wide, buf_hbm, inst, trow,
    acc, pall, irow, istat,
    buf, timed, tback, aback, stage, qs, ks, vs, os, arow, part, partbf, pgot, pnew,
    ipart, igot, tsend, trecv, asend, arecv, own_sem, zsend, zrecv, load_sem,
):
    me = lax.axis_index("st")
    mz = lax.axis_index("ha")
    hello("st", 32)
    hello("ha", 8)
    load = pltpu.make_async_copy(wide, acc, load_sem.at[0])
    load.start()
    load_flat = pltpu.make_async_copy(buf_hbm, buf, load_sem.at[1])
    load_flat.start()

    def to_st(src, dst, send, recv, i, peer):
        copy = pltpu.make_async_remote_copy(
            src_ref=src,
            dst_ref=dst,
            send_sem=send.at[i],
            recv_sem=recv.at[i],
            device_id={"st": peer},
            device_id_type=MESH,
        )
        copy.start()
        return copy

    def return_half(half):
        copies = [
            to_st(
                timed.at[half, peer_to(me, move)], tback.at[half, me],
                tsend.at[half], trecv.at[half], i, peer_to(me, move),
            )
            for i, move in enumerate(MOVES)
        ]
        own = pltpu.make_async_copy(
            timed.at[half, me], tback.at[half, me], own_sem.at[half]
        )
        own.start()
        return copies + [own]

    known = mask[...]
    time_half(patch, known, 0, stage, qs, ks, vs, os, timed)
    greeted(38)
    answers = []
    for i, move in enumerate(MOVES):
        peer = peer_to(me, move)
        answers.append(
            to_st(
                ans.at[rows_at(peer * 32, 32)], aback.at[rows_at(me * 32, 32)],
                asend, arecv, i, peer,
            )
        )
    own = pltpu.make_async_copy(
        ans.at[rows_at(me * 32, 32)], aback.at[rows_at(me * 32, 32)], own_sem.at[2]
    )
    own.start()
    answers.append(own)
    backs = return_half(0)
    time_half(patch, known, 1, stage, qs, ks, vs, os, timed)
    backs = backs + return_half(1)

    load.wait()
    load_flat.wait()
    width_all(buf, acc, 16)

    def exchange(src, dst, at_src, at_dst, which):
        copies = []
        for s in range(1, 8):
            peer = lax.rem(mz + s, 8)
            copy = pltpu.make_async_remote_copy(
                src_ref=at_src(src, peer),
                dst_ref=at_dst(dst),
                send_sem=zsend.at[which, s],
                recv_sem=zrecv.at[which, s],
                device_id={"ha": peer},
                device_id_type=MESH,
            )
            copy.start()
            copies.append(copy)
        return copies

    arrival, place = slots_of(trow[...])
    for copy in answers:
        copy.wait()
    arow[...] = aback[...].astype(F32)
    for r in range(16):
        mine = lax.dot_general(
            arow[pl.ds(r, 64, stride=16), :].astype(BF),
            place,
            (((0,), (0,)), ((), ())),
            preferred_element_type=F32,
        )
        pre = inst[r].astype(F32)
        for j in range(4):
            pre = pre + jnp.where(arrival == j, mine[j * 32 : (j + 1) * 32], 0.0)
        irow[r] = pre
        ipart[pl.ds(r, 1), :] = jnp.sum(pre, axis=0, keepdims=True)
        ipart[pl.ds(16 + r, 1), :] = jnp.sum(pre * pre, axis=0, keepdims=True)
    shared = exchange(ipart, igot, lambda a, p: a, lambda a: a.at[mz], 0)
    igot[mz] = ipart[...]

    for copy in backs:
        copy.wait()

    def add_time(d, _):
        for half in range(2):
            r = pl.ds(d * 2 + half, 64, stride=64)
            acc[r, :] = acc[r, :] + tback[half, d].astype(F32)
        return 0

    lax.fori_loop(0, 32, add_time, 0, unroll=4)
    for f in range(2):

        def sums(c, carry):
            x = acc[rows_at(f * 2048 + c * 64, 64), :]
            return carry[0] + x, carry[1] + x * x

        zero = jnp.zeros((64, 128), F32)
        tot, sqr = lax.fori_loop(0, 32, sums, (zero, zero), unroll=4)
        for b in range(4):
            part[f * 4 + b, 0:16, :] = tot[b * 16 : (b + 1) * 16]
            part[f * 4 + b, 16:32, :] = sqr[b * 16 : (b + 1) * 16]
    partbf[...] = part[...].astype(BF)
    scattered = exchange(partbf, pgot, lambda a, p: a.at[p], lambda a: a.at[mz], 1)
    pgot[mz] = partbf[mz]
    for copy in shared:
        copy.wait()
    total = igot[0]
    for z in range(1, 8):
        total = total + igot[z]
    mean = total[:16] / C
    istat[0:16, :] = mean
    istat[16:32, :] = lax.rsqrt(total[16:] / C - mean * mean + EPSILON)
    for copy in scattered:
        copy.wait()
    total = pgot[0].astype(F32)
    for z in range(1, 8):
        total = total + pgot[z].astype(F32)
    mean = total[:16] / C
    pnew[0:16, :] = mean.astype(BF)
    pnew[16:32, :] = lax.rsqrt(total[16:] / C - mean * mean + EPSILON).astype(BF)
    gathered = exchange(pnew, pall, lambda a, p: a, lambda a: a.at[mz], 2)
    pall[mz] = pnew[...]
    for copy in gathered:
        copy.wait()


def last(patch, mask, ans, wide, buf, inst, trow):
    sd = jax.ShapeDtypeStruct
    dma = pltpu.SemaphoreType.DMA
    return pl.pallas_call(
        last_kernel,
        out_shape=(
            sd((4096, 128), F32),
            sd((8, 32, 128), BF),
            sd((16, 32, 128), F32),
            sd((32, 128), F32),
        ),
        in_specs=[VM] * 2 + [HB] * 3 + [VM] * 2,
        out_specs=(VM, VM, VM, VM),
        scratch_shapes=[
            pltpu.VMEM((32, 192, 256), BF),
            pltpu.VMEM((2, 32, 64, 128), BF),
            pltpu.VMEM((2, 32, 64, 128), BF),
            pltpu.VMEM((1024, 128), BF),
            pltpu.VMEM((2048, 128), F32),
            pltpu.VMEM((2048, 128), F32),
            pltpu.VMEM((2048, 128), F32),
            pltpu.VMEM((2048, 128), F32),
            pltpu.VMEM((2048, 128), F32),
            pltpu.VMEM((1024, 128), F32),
            pltpu.VMEM((8, 32, 128), F32),
            pltpu.VMEM((8, 32, 128), BF),
            pltpu.VMEM((8, 32, 128), BF),
            pltpu.VMEM((32, 128), BF),
            pltpu.VMEM((32, 128), F32),
            pltpu.VMEM((8, 32, 128), F32),
            dma((2, 31)),
            dma((2, 31)),
            dma((31,)),
            dma((31,)),
            dma((3,)),
            dma((3, 8)),
            dma((3, 8)),
            dma((2,)),
        ],
        compiler_params=pltpu.CompilerParams(
            collective_id=1, has_side_effects=True, vmem_limit_bytes=60 << 20
        ),
        cost_estimate=pl.CostEstimate(
            flops=1 << 32, bytes_accessed=12 << 20, transcendentals=1 << 21
        ),
    )(patch, mask, ans, wide, buf, inst, trow)


def norm_kernel(
    acc_hbm, pall_hbm, irow_hbm, istat_hbm, qrow, pgain, igain, pixel_hbm, inst_out,
    acc, pall, irow, istat, pixel_out, sem,
):
    loads = [
        pltpu.make_async_copy(pall_hbm, pall, sem.at[0]),
        pltpu.make_async_copy(acc_hbm.at[pl.ds(0, 2048)], acc.at[pl.ds(0, 2048)], sem.at[1]),
        pltpu.make_async_copy(
            acc_hbm.at[pl.ds(2048, 2048)], acc.at[pl.ds(2048, 2048)], sem.at[2]
        ),
        pltpu.make_async_copy(istat_hbm, istat, sem.at[3]),
        pltpu.make_async_copy(irow_hbm, irow, sem.at[4]),
    ]
    for load in loads:
        load.start()
    loads[0].wait()
    saves = []
    for f in range(2):
        loads[1 + f].wait()

        def finish(c, _):
            r = rows_at(f * 2048 + c * 64, 64)
            gain = pgain[c]
            x = acc[r, :]
            for b in range(4):
                low = slice(b * 16, (b + 1) * 16)
                known = pall[f * 4 + b].astype(F32)
                y = (x[low] - known[:16]) * known[16:] * gain
                pixel_out[f, c, low, :] = y.astype(BF)
            return 0

        lax.fori_loop(0, 32, finish, 0, unroll=4)
        save = pltpu.make_async_copy(pixel_out.at[f], pixel_hbm.at[f], sem.at[5 + f])
        save.start()
        saves.append(save)
    loads[3].wait()
    loads[4].wait()
    row = igain[...]
    gains = columns_of(jnp.concatenate([row, row, row, row], axis=1))[:32]
    live = qrow[...]
    for r in range(16):
        y = (irow[r] - istat[pl.ds(r, 1), :]) * istat[pl.ds(16 + r, 1), :] * gains
        inst_out[r] = jnp.where(live > r, y, 0.0).astype(BF)
    for save in saves:
        save.wait()


def norm(acc, pall, irow, istat, qrow, pgain, igain):
    sd = jax.ShapeDtypeStruct
    return pl.pallas_call(
        norm_kernel,
        out_shape=(sd((2, 32, 64, 128), BF), sd((16, 32, 128), BF)),
        in_specs=[HB] * 4 + [VM, SM, VM],
        out_specs=(HB, VM),
        scratch_shapes=[
            pltpu.VMEM((4096, 128), F32),
            pltpu.VMEM((8, 32, 128), BF),
            pltpu.VMEM((16, 32, 128), F32),
            pltpu.VMEM((32, 128), F32),
            pltpu.VMEM((2, 32, 64, 128), BF),
            pltpu.SemaphoreType.DMA((7,)),
        ],
        compiler_params=pltpu.CompilerParams(vmem_limit_bytes=60 << 20),
        cost_estimate=pl.CostEstimate(flops=1 << 22, bytes_accessed=3 << 20, transcendentals=0),
    )(acc, pall, irow, istat, qrow, pgain, igain)


def per_device(
    clip_lengths,
    inst_frame,
    query_rows,
    pix_q,
    pix_k,
    pix_v,
    features,
    pixel_gain,
    inst_query,
    inst_gain,
):
    clip_ends = jnp.cumsum(clip_lengths)
    frame_ids = jnp.arange(64, dtype=jnp.int32)
    clip_of = jnp.sum((clip_ends[None, :] <= frame_ids[:, None]).astype(jnp.int32), axis=1)
    same_clip = clip_of[:, None] == clip_of[None, :]
    mask = jnp.where(same_clip, 0.0, MASKED).astype(F32)
    mask = jnp.concatenate([mask, mask], axis=1)
    trow = inst_frame.reshape(1, 128)
    qrow = query_rows.reshape(1, 128)
    inst = inst_query.transpose(1, 2, 0)
    buf, kflat, got = first(pix_q, pix_k, pix_v, inst, trow, qrow)
    buf, got = lax.optimization_barrier((buf, got))
    patch = lax.all_to_all(buf, "st", split_axis=0, concat_axis=0, tiled=True)
    ans, wide = middle(got, kflat, buf, pix_q, pix_k, pix_v, features)
    acc, pall, irow, istat = last(patch, mask, ans, wide, buf, inst, trow)
    pixel_out, inst_out = norm(
        acc, pall, irow, istat, qrow, pixel_gain, inst_gain.reshape(1, 32)
    )
    return pixel_out, inst_out.transpose(2, 0, 1)


def solution(mesh):
    placed = (
        P(),
        P("st", None),
        P("st"),
        P("st", "ha", None, None),
        P("st", "ha", None, None),
        P("st", "ha", None, None),
        P("st", "ha", None, None),
        P("ha"),
        P("st", None, "ha"),
        P("ha"),
    )
    return jax.shard_map(
        per_device,
        mesh=mesh,
        in_specs=placed,
        out_specs=(P("st", "ha", None, None), P("st", None, "ha")),
        check_vma=False,
    )
```

```python
import jax
import jax.numpy as jnp
from jax import lax
from jax.experimental import pallas as pl
from jax.experimental.pallas import tpu as pltpu
from jax.sharding import PartitionSpec as P

F32 = jnp.float32
BF = jnp.bfloat16
MESH = pl.DeviceIdType.MESH
C = 256
HD = 32
EPSILON = 1e-05
MASKED = -1e30
SCALE2 = (HD**-0.5) * 1.4426950408889634
DEAD = 16384.0
CHUNK = 2048
BIG, SMALL = 512, 128
QROWS = 2048 + BIG
VM = pl.BlockSpec(memory_space=pltpu.VMEM)
SM = pl.BlockSpec(memory_space=pltpu.SMEM)
HB = pl.BlockSpec(memory_space=pltpu.HBM)


def rows_at(start, size):
    return pl.ds(pl.multiple_of(start, size), size)


def scores_of(k, q):
    return lax.dot_general(k, q, (((0,), (0,)), ((), ())), preferred_element_type=F32)


def width_step(q, k, v):
    s = scores_of(k, q) * SCALE2
    e = jnp.exp2(s - jnp.max(s, axis=0, keepdims=True))
    total = jnp.sum(e, axis=0, keepdims=True)
    return jnp.dot(v, e.astype(BF), preferred_element_type=F32) * (1.0 / total)


def pair_step(q, k, v, low, mask):
    s = scores_of(k, q)
    s = jnp.where(low, s[:64], s[64:]) * SCALE2
    if mask is not None:
        s = s + mask
    e = jnp.exp2(s - jnp.max(s, axis=0, keepdims=True))
    total = jnp.sum(e, axis=0, keepdims=True)
    zero = jnp.zeros_like(e)
    p = jnp.concatenate([jnp.where(low, e, zero), jnp.where(low, zero, e)], axis=0)
    return jnp.dot(v, p.astype(BF), preferred_element_type=F32) * (1.0 / total)


def attend_pairs(qs, ks, vs, os, mask, count, unroll):
    low = lax.broadcasted_iota(jnp.int32, (64, 128), 1) < 64

    def body(b, _):
        r = rows_at(b * 32, 32)
        os[r, :] = pair_step(
            qs[r, :].astype(BF), ks[r, :].astype(BF), vs[r, :].astype(BF), low, mask
        )
        return 0

    lax.fori_loop(0, count, body, 0, unroll=unroll)


def width_all(buf, acc, unroll):
    for f in range(2):

        def body(d, _):
            for half in range(2):
                lanes = pl.ds(half * 128, 128)
                o = width_step(
                    buf[d, pl.ds(f * 32, 32), lanes],
                    buf[d, pl.ds(64 + f * 32, 32), lanes],
                    buf[d, pl.ds(128 + f * 32, 32), lanes],
                )
                r = pl.ds(f * 2048 + d * 2 + half, 32, stride=64)
                acc[r, :] = acc[r, :] + o
            return 0

        lax.fori_loop(0, 32, body, 0, unroll=unroll)


def height_in(src, dst):
    def body(c, _):
        t = jnp.concatenate([src[0, c], src[1, c]], axis=0).astype(F32)
        dst[pl.ds(c, 128, stride=32), :] = t.T
        return 0

    lax.fori_loop(0, 32, body, 0, unroll=4)


def height_out(os, features, acc):
    def body(c, _):
        t = os[pl.ds(c, 128, stride=32), :].T
        for f in range(2):
            r = rows_at(f * 2048 + c * 64, 64)
            acc[r, :] = t[f * 64 : (f + 1) * 64] + features[f, c].astype(F32)
        return 0

    lax.fori_loop(0, 32, body, 0, unroll=4)


BASE = (
    (1, 0), (0, 1), (3, 0), (0, 3), (2, 0), (0, 2), (1, 1), (3, 3),
    (1, 3), (3, 1), (2, 1), (1, 2), (2, 3), (3, 2), (2, 2),
)
MOVES = tuple((a, b, c) for a, b in BASE for c in (0, 1)) + ((0, 0, 1),)


def peer_to(me, move):
    dx, dy, dc = move
    x, y, core = me // 8, (me // 2) % 4, me % 2
    sx = dx + core * ((4 - 2 * dx) % 4)
    sy = dy + core * ((4 - 2 * dy) % 4)
    return ((x + sx) % 4) * 8 + ((y + sy) % 4) * 2 + (core + dc) % 2


def hello(axis, size):
    me = lax.axis_index(axis)
    barrier = pltpu.get_barrier_semaphore()

    def signal(s, _):
        pl.semaphore_signal(
            barrier, inc=1, device_id={axis: lax.rem(me + s, size)}, device_id_type=MESH
        )
        return 0

    lax.fori_loop(1, size, signal, 0)


def greeted(total):
    pl.semaphore_wait(pltpu.get_barrier_semaphore(), total)


def columns_of(row):
    return jnp.broadcast_to(row, (128, 128)).T


def slots_of(trow):
    target = trow.astype(F32)
    one = lax.broadcasted_iota(jnp.int32, (128, 128), 0)
    two = lax.broadcasted_iota(jnp.int32, (128, 128), 1)
    before = jnp.where((columns_of(target) == target) & (one < two), 1.0, 0.0)
    arrival = jnp.sum(before, axis=0, keepdims=True)
    frame = lax.broadcasted_iota(jnp.int32, (64, 128), 0)
    return arrival, jnp.where(frame == trow, 1.0, 0.0).astype(BF)


def first_kernel(
    q, k, v, inst_hbm, trow, qrow, buf_hbm, kflat_hbm, got,
    stage, rows, msg, raw, inst, buf, kflat,
    send_sem, recv_sem, own_sem, load_sem, save_sem,
):
    me = lax.axis_index("st")
    load_inst = pltpu.make_async_copy(inst_hbm, inst, load_sem.at[3])
    load_inst.start()
    loads = []
    for number, src in enumerate((k, v, q)):
        load = pltpu.make_async_copy(src, raw.at[number], load_sem.at[number])
        load.start()
        loads.append(load)
    hello("st", 32)
    arrival, place = slots_of(trow[...])
    live = qrow[...].astype(F32)
    group = lax.broadcasted_iota(jnp.int32, (128, 128), 0) // 32
    here = group.astype(F32) == arrival
    counts = lax.dot_general(
        place,
        jnp.where(here, live, 0.0).astype(BF),
        (((1,), (1,)), ((), ())),
        preferred_element_type=F32,
    )
    load_inst.wait()
    for r in range(16):
        x = inst[r].astype(F32)
        y = jnp.where(here, jnp.concatenate([x, x, x, x], axis=0), 0.0).astype(BF)
        put = lax.dot_general(
            place, y, (((1,), (1,)), ((), ())), preferred_element_type=F32
        )
        rows[pl.ds(r, 64, stride=16), :] = jnp.where(counts > r + 0.5, put, DEAD)
    msg[...] = rows[...].astype(BF)
    greeted(31)
    copies = []
    for i, move in enumerate(MOVES):
        peer = peer_to(me, move)
        copy = pltpu.make_async_remote_copy(
            src_ref=msg.at[rows_at(peer * 32, 32)],
            dst_ref=got.at[rows_at(me * 32, 32)],
            send_sem=send_sem.at[i],
            recv_sem=recv_sem.at[i],
            device_id={"st": peer},
            device_id_type=MESH,
        )
        copy.start()
        copies.append(copy)
    own = pltpu.make_async_copy(
        msg.at[rows_at(me * 32, 32)], got.at[rows_at(me * 32, 32)], own_sem
    )
    own.start()
    saves = []
    for number in range(3):
        base = (64, 128, 0)[number]
        loads[number].wait()

        def widen(c, _):
            for f in range(2):
                stage[rows_at(f * 2048 + c * 64, 64), :] = raw[number, f, c].astype(F32)
            return 0

        lax.fori_loop(0, 32, widen, 0, unroll=4)

        def body(d, _):
            for half in range(2):
                x = stage[pl.ds(d * 2 + half, 64, stride=64), :].astype(BF)
                buf[d, pl.ds(base, 64), pl.ds(half * 128, 128)] = x
                if number == 0:
                    kflat[:, rows_at((d * 2 + half) * 128, 128)] = x
            return 0

        lax.fori_loop(0, 32, body, 0, unroll=4)
        part = pl.ds(base, 64)
        save = pltpu.make_async_copy(
            buf.at[:, part, :], buf_hbm.at[:, part, :], save_sem.at[number]
        )
        save.start()
        saves.append(save)
        if number == 0:
            save = pltpu.make_async_copy(kflat, kflat_hbm, save_sem.at[3])
            save.start()
            saves.append(save)
    for save in saves:
        save.wait()
    own.wait()
    for copy in copies:
        copy.wait()


def first(q, k, v, inst, trow, qrow):
    sd = jax.ShapeDtypeStruct
    dma = pltpu.SemaphoreType.DMA
    return pl.pallas_call(
        first_kernel,
        out_shape=(sd((32, 192, 256), BF), sd((64, 8192), BF), sd((1024, 128), BF)),
        in_specs=[HB] * 4 + [VM] * 2,
        out_specs=(HB, HB, HB),
        scratch_shapes=[
            pltpu.VMEM((4096, 128), F32),
            pltpu.VMEM((1024, 128), F32),
            pltpu.VMEM((1024, 128), BF),
            pltpu.VMEM((3, 2, 32, 64, 128), BF),
            pltpu.VMEM((16, 32, 128), BF),
            pltpu.VMEM((32, 192, 256), BF),
            pltpu.VMEM((64, 8192), BF),
            dma((31,)),
            dma((31,)),
            dma,
            dma((4,)),
            dma((4,)),
        ],
        compiler_params=pltpu.CompilerParams(
            collective_id=0, has_side_effects=True, vmem_limit_bytes=60 << 20
        ),
        cost_estimate=pl.CostEstimate(flops=1 << 24, bytes_accessed=8 << 20, transcendentals=0),
    )(q, k, v, inst, trow, qrow)


def cross_block(q, kflat, values, f):
    most, acc = None, None
    for j in range(8192 // CHUNK):
        s = jnp.dot(
            q,
            kflat[f * 32 : (f + 1) * 32, j * CHUNK : (j + 1) * CHUNK],
            preferred_element_type=F32,
        )
        here = jnp.max(s, axis=1, keepdims=True) * SCALE2
        new = here if most is None else jnp.maximum(most, here)
        p = jnp.exp2(s * SCALE2 - new).astype(BF)
        o = jnp.dot(p, values[pl.ds(j * CHUNK, CHUNK), :], preferred_element_type=F32)
        acc = o if acc is None else acc * jnp.exp2(most - new) + o
        most = new
    return acc / acc[:, 64:65]


def middle_kernel(
    got_hbm, kflat_hbm, buf_hbm, q, k, v, features, ans_hbm, wide_hbm,
    got, kflat, buf, raw, ans, acc, qs, ks, vs, os,
    values, wide, packed, solved, live, counts, starts, sem,
):
    pairs = ((got_hbm, got), (buf_hbm, buf)) + tuple(
        (src, raw.at[i]) for i, src in enumerate((q, k, v, features))
    ) + ((kflat_hbm, kflat),)
    loads = [pltpu.make_async_copy(x, y, sem.at[i]) for i, (x, y) in enumerate(pairs)]
    for load in loads:
        load.start()
    loads[0].wait()
    wide[...] = got[...].astype(F32)
    alive = jnp.where(wide[...] < DEAD / 2, 1.0, 0.0).reshape(64, 16, 128)
    live[...] = jnp.sum(alive, axis=1).astype(jnp.int32)
    down = pltpu.make_async_copy(live, counts, sem.at[7])
    down.start()
    loads[1].wait()

    def turn(d, _):
        t = buf[d, pl.ds(128, 64), :].astype(F32)
        full = jnp.concatenate([t, jnp.ones((64, 256), F32)], axis=0)
        values[rows_at(d * 256, 256), :] = full.T.astype(BF)
        return 0

    lax.fori_loop(0, 32, turn, 0, unroll=2)
    for load in loads[2:]:
        load.wait()
    height_in(raw.at[0], qs)
    height_in(raw.at[1], ks)
    height_in(raw.at[2], vs)
    attend_pairs(qs, ks, vs, os, None, 128, 32)
    height_out(os, raw.at[3], acc)
    save = pltpu.make_async_copy(acc, wide_hbm, sem.at[8])
    save.start()
    down.wait()

    for f in range(2):

        def pack(src, offset):
            block = wide[pl.ds(pl.multiple_of(src * 32 + f * 16, 16), 16), :]
            for j in range(4):
                starts[src * 2 + f, j] = offset
                moved = block if j == 0 else pltpu.roll(block, 128 - 32 * j, 1)
                packed[pl.ds(offset, 16), :] = moved
                offset = offset + counts[src * 2 + f, 32 * j]
            return offset

        total = lax.fori_loop(0, 32, pack, 0, unroll=4)
        many = (total + SMALL - 1) // BIG
        rest = jnp.maximum(total - many * BIG, 0)

        def big(b, _):
            r = rows_at(b * BIG, BIG)
            solved[r, :] = cross_block(packed[r, :][:, :32].astype(BF), kflat, values, f)
            return 0

        lax.fori_loop(0, many, big, 0)

        def small(b, _):
            r = rows_at(many * BIG + b * SMALL, SMALL)
            solved[r, :] = cross_block(packed[r, :][:, :32].astype(BF), kflat, values, f)
            return 0

        lax.fori_loop(0, (rest + SMALL - 1) // SMALL, small, 0)
        row = lax.broadcasted_iota(jnp.int32, (16, 128), 0)
        group = lax.broadcasted_iota(jnp.int32, (16, 128), 1) // 32

        def unpack(src, _):
            out = jnp.zeros((16, 128), F32)
            for j in range(4):
                x = solved[pl.ds(starts[src * 2 + f, j], 16), :]
                shift = (32 * (j - f)) % 128
                moved = x if shift == 0 else pltpu.roll(x, shift, 1)
                keep = (group == j) & (row < counts[src * 2 + f, 32 * j])
                out = jnp.where(keep, moved, out)
            ans[pl.ds(pl.multiple_of(src * 32 + f * 16, 16), 16), :] = out.astype(BF)
            return 0

        lax.fori_loop(0, 32, unpack, 0, unroll=4)
    back = pltpu.make_async_copy(ans, ans_hbm, sem.at[9])
    back.start()
    back.wait()
    save.wait()


def middle(got, kflat, buf, q, k, v, features):
    sd = jax.ShapeDtypeStruct
    return pl.pallas_call(
        middle_kernel,
        out_shape=(sd((1024, 128), BF), sd((4096, 128), F32)),
        in_specs=[HB] * 7,
        out_specs=(HB, HB),
        scratch_shapes=[
            pltpu.VMEM((1024, 128), BF),
            pltpu.VMEM((64, 8192), BF),
            pltpu.VMEM((32, 192, 256), BF),
            pltpu.VMEM((4, 2, 32, 64, 128), BF),
            pltpu.VMEM((1024, 128), BF),
            pltpu.VMEM((4096, 128), F32),
            pltpu.VMEM((4096, 128), F32),
            pltpu.VMEM((4096, 128), F32),
            pltpu.VMEM((4096, 128), F32),
            pltpu.VMEM((4096, 128), F32),
            pltpu.VMEM((8192, 128), BF),
            pltpu.VMEM((1024, 128), F32),
            pltpu.VMEM((QROWS, 128), F32),
            pltpu.VMEM((QROWS, 128), F32),
            pltpu.VMEM((64, 128), jnp.int32),
            pltpu.SMEM((64, 128), jnp.int32),
            pltpu.SMEM((64, 4), jnp.int32),
            pltpu.SemaphoreType.DMA((10,)),
        ],
        compiler_params=pltpu.CompilerParams(vmem_limit_bytes=60 << 20),
        cost_estimate=pl.CostEstimate(
            flops=17 << 30, bytes_accessed=8 << 20, transcendentals=1 << 24
        ),
    )(got, kflat, buf, q, k, v, features)


def time_half(patch, mask, half, stage, qs, ks, vs, os, out, between):
    low = lax.broadcasted_iota(jnp.int32, (64, 128), 1) < 64
    lanes = pl.ds(half * 128, 128)
    for base, dst in ((0, qs), (64, ks), (128, vs)):

        def spread(i, _):
            stage[rows_at(i * 64, 64), :] = patch[i, pl.ds(base, 64), lanes].astype(F32)
            return 0

        lax.fori_loop(0, 32, spread, 0, unroll=4)

        def turn(b, _):
            one, two = pl.ds(b * 2, 64, stride=32), pl.ds(b * 2 + 1, 64, stride=32)
            t = jnp.concatenate([stage[one, :], stage[two, :]], axis=0).T
            top, end = t[:64], t[64:]
            dst[one, :] = jnp.where(low, top, pltpu.roll(end, 64, 1))
            dst[two, :] = jnp.where(low, pltpu.roll(top, 64, 1), end)
            return 0

        lax.fori_loop(0, 16, turn, 0, unroll=4)
    between()
    attend_pairs(qs, ks, vs, os, mask, 64, 32)

    def turn_back(b, _):
        one, two = pl.ds(b * 2, 64, stride=32), pl.ds(b * 2 + 1, 64, stride=32)
        x, y = os[one, :], os[two, :]
        top = jnp.where(low, x, pltpu.roll(y, 64, 1))
        end = jnp.where(low, pltpu.roll(x, 64, 1), y)
        t = jnp.concatenate([top, end], axis=0).T
        stage[one, :] = t[:64]
        stage[two, :] = t[64:]
        return 0

    lax.fori_loop(0, 16, turn_back, 0, unroll=4)

    def gather(i, _):
        out[half, i] = stage[rows_at(i * 64, 64), :].astype(BF)
        return 0

    lax.fori_loop(0, 32, gather, 0, unroll=4)


def last_kernel(
    patch, mask, ans, wide, buf_hbm, inst, trow,
    acc, pall, irow, istat,
    buf, timed, tback, aback, stage, qs, ks, vs, os, arow, part, partbf, pgot, pnew,
    ipart, igot, tsend, trecv, asend, arecv, own_sem, zsend, zrecv, load_sem,
):
    me = lax.axis_index("st")
    mz = lax.axis_index("ha")
    hello("st", 32)
    hello("ha", 8)
    load = pltpu.make_async_copy(wide, acc, load_sem.at[0])
    load.start()
    load_flat = pltpu.make_async_copy(buf_hbm, buf, load_sem.at[1])
    load_flat.start()

    def to_st(src, dst, send, recv, i, peer):
        copy = pltpu.make_async_remote_copy(
            src_ref=src,
            dst_ref=dst,
            send_sem=send.at[i],
            recv_sem=recv.at[i],
            device_id={"st": peer},
            device_id_type=MESH,
        )
        copy.start()
        return copy

    def return_half(half):
        copies = [
            to_st(
                timed.at[half, peer_to(me, move)], tback.at[half, me],
                tsend.at[half], trecv.at[half], i, peer_to(me, move),
            )
            for i, move in enumerate(MOVES)
        ]
        own = pltpu.make_async_copy(
            timed.at[half, me], tback.at[half, me], own_sem.at[half]
        )
        own.start()
        return copies + [own]

    known = mask[...]
    answers = []

    def send_answers():
        greeted(38)
        for i, move in enumerate(MOVES):
            peer = peer_to(me, move)
            answers.append(
                to_st(
                    ans.at[rows_at(peer * 32, 32)], aback.at[rows_at(me * 32, 32)],
                    asend, arecv, i, peer,
                )
            )
        own = pltpu.make_async_copy(
            ans.at[rows_at(me * 32, 32)], aback.at[rows_at(me * 32, 32)], own_sem.at[2]
        )
        own.start()
        answers.append(own)

    time_half(patch, known, 0, stage, qs, ks, vs, os, timed, send_answers)
    backs = return_half(0)
    time_half(patch, known, 1, stage, qs, ks, vs, os, timed, lambda: None)
    backs = backs + return_half(1)

    load.wait()
    load_flat.wait()
    width_all(buf, acc, 16)

    def exchange(src, dst, at_src, at_dst, which):
        copies = []
        for s in range(1, 8):
            peer = lax.rem(mz + s, 8)
            copy = pltpu.make_async_remote_copy(
                src_ref=at_src(src, peer),
                dst_ref=at_dst(dst),
                send_sem=zsend.at[which, s],
                recv_sem=zrecv.at[which, s],
                device_id={"ha": peer},
                device_id_type=MESH,
            )
            copy.start()
            copies.append(copy)
        return copies

    arrival, place = slots_of(trow[...])
    for copy in answers:
        copy.wait()
    arow[...] = aback[...].astype(F32)
    for r in range(16):
        mine = lax.dot_general(
            arow[pl.ds(r, 64, stride=16), :].astype(BF),
            place,
            (((0,), (0,)), ((), ())),
            preferred_element_type=F32,
        )
        pre = inst[r].astype(F32)
        for j in range(4):
            pre = pre + jnp.where(arrival == j, mine[j * 32 : (j + 1) * 32], 0.0)
        irow[r] = pre
        ipart[pl.ds(r, 1), :] = jnp.sum(pre, axis=0, keepdims=True)
        ipart[pl.ds(16 + r, 1), :] = jnp.sum(pre * pre, axis=0, keepdims=True)
    shared = exchange(ipart, igot, lambda a, p: a, lambda a: a.at[mz], 0)
    igot[mz] = ipart[...]

    for copy in backs:
        copy.wait()

    def add_time(d, _):
        for half in range(2):
            r = pl.ds(d * 2 + half, 64, stride=64)
            acc[r, :] = acc[r, :] + tback[half, d].astype(F32)
        return 0

    lax.fori_loop(0, 32, add_time, 0, unroll=4)
    for f in range(2):

        def sums(c, carry):
            x = acc[rows_at(f * 2048 + c * 64, 64), :]
            return carry[0] + x, carry[1] + x * x

        zero = jnp.zeros((64, 128), F32)
        tot, sqr = lax.fori_loop(0, 32, sums, (zero, zero), unroll=4)
        for b in range(4):
            part[f * 4 + b, 0:16, :] = tot[b * 16 : (b + 1) * 16]
            part[f * 4 + b, 16:32, :] = sqr[b * 16 : (b + 1) * 16]
    partbf[...] = part[...].astype(BF)
    scattered = exchange(partbf, pgot, lambda a, p: a.at[p], lambda a: a.at[mz], 1)
    pgot[mz] = partbf[mz]
    for copy in shared:
        copy.wait()
    total = igot[0]
    for z in range(1, 8):
        total = total + igot[z]
    mean = total[:16] / C
    istat[0:16, :] = mean
    istat[16:32, :] = lax.rsqrt(total[16:] / C - mean * mean + EPSILON)
    for copy in scattered:
        copy.wait()
    total = pgot[0].astype(F32)
    for z in range(1, 8):
        total = total + pgot[z].astype(F32)
    mean = total[:16] / C
    pnew[0:16, :] = mean.astype(BF)
    pnew[16:32, :] = lax.rsqrt(total[16:] / C - mean * mean + EPSILON).astype(BF)
    gathered = exchange(pnew, pall, lambda a, p: a, lambda a: a.at[mz], 2)
    pall[mz] = pnew[...]
    for copy in gathered:
        copy.wait()


def last(patch, mask, ans, wide, buf, inst, trow):
    sd = jax.ShapeDtypeStruct
    dma = pltpu.SemaphoreType.DMA
    return pl.pallas_call(
        last_kernel,
        out_shape=(
            sd((4096, 128), F32),
            sd((8, 32, 128), BF),
            sd((16, 32, 128), F32),
            sd((32, 128), F32),
        ),
        in_specs=[VM] * 2 + [HB] * 3 + [VM] * 2,
        out_specs=(VM, VM, VM, VM),
        scratch_shapes=[
            pltpu.VMEM((32, 192, 256), BF),
            pltpu.VMEM((2, 32, 64, 128), BF),
            pltpu.VMEM((2, 32, 64, 128), BF),
            pltpu.VMEM((1024, 128), BF),
            pltpu.VMEM((2048, 128), F32),
            pltpu.VMEM((2048, 128), F32),
            pltpu.VMEM((2048, 128), F32),
            pltpu.VMEM((2048, 128), F32),
            pltpu.VMEM((2048, 128), F32),
            pltpu.VMEM((1024, 128), F32),
            pltpu.VMEM((8, 32, 128), F32),
            pltpu.VMEM((8, 32, 128), BF),
            pltpu.VMEM((8, 32, 128), BF),
            pltpu.VMEM((32, 128), BF),
            pltpu.VMEM((32, 128), F32),
            pltpu.VMEM((8, 32, 128), F32),
            dma((2, 31)),
            dma((2, 31)),
            dma((31,)),
            dma((31,)),
            dma((3,)),
            dma((3, 8)),
            dma((3, 8)),
            dma((2,)),
        ],
        compiler_params=pltpu.CompilerParams(
            collective_id=1, has_side_effects=True, vmem_limit_bytes=60 << 20
        ),
        cost_estimate=pl.CostEstimate(
            flops=1 << 32, bytes_accessed=12 << 20, transcendentals=1 << 21
        ),
    )(patch, mask, ans, wide, buf, inst, trow)


def norm_kernel(
    acc_hbm, pall_hbm, irow_hbm, istat_hbm, qrow, pgain, igain, pixel_hbm, inst_out,
    acc, pall, irow, istat, pixel_out, sem,
):
    loads = [
        pltpu.make_async_copy(pall_hbm, pall, sem.at[0]),
        pltpu.make_async_copy(acc_hbm.at[pl.ds(0, 2048)], acc.at[pl.ds(0, 2048)], sem.at[1]),
        pltpu.make_async_copy(
            acc_hbm.at[pl.ds(2048, 2048)], acc.at[pl.ds(2048, 2048)], sem.at[2]
        ),
        pltpu.make_async_copy(istat_hbm, istat, sem.at[3]),
        pltpu.make_async_copy(irow_hbm, irow, sem.at[4]),
    ]
    for load in loads:
        load.start()
    loads[0].wait()
    saves = []
    for f in range(2):
        loads[1 + f].wait()

        def finish(c, _):
            r = rows_at(f * 2048 + c * 64, 64)
            gain = pgain[c]
            x = acc[r, :]
            for b in range(4):
                low = slice(b * 16, (b + 1) * 16)
                known = pall[f * 4 + b].astype(F32)
                y = (x[low] - known[:16]) * known[16:] * gain
                pixel_out[f, c, low, :] = y.astype(BF)
            return 0

        lax.fori_loop(0, 32, finish, 0, unroll=4)
        save = pltpu.make_async_copy(pixel_out.at[f], pixel_hbm.at[f], sem.at[5 + f])
        save.start()
        saves.append(save)
    loads[3].wait()
    loads[4].wait()
    row = igain[...]
    gains = columns_of(jnp.concatenate([row, row, row, row], axis=1))[:32]
    live = qrow[...]
    for r in range(16):
        y = (irow[r] - istat[pl.ds(r, 1), :]) * istat[pl.ds(16 + r, 1), :] * gains
        inst_out[r] = jnp.where(live > r, y, 0.0).astype(BF)
    for save in saves:
        save.wait()


def norm(acc, pall, irow, istat, qrow, pgain, igain):
    sd = jax.ShapeDtypeStruct
    return pl.pallas_call(
        norm_kernel,
        out_shape=(sd((2, 32, 64, 128), BF), sd((16, 32, 128), BF)),
        in_specs=[HB] * 4 + [VM, SM, VM],
        out_specs=(HB, VM),
        scratch_shapes=[
            pltpu.VMEM((4096, 128), F32),
            pltpu.VMEM((8, 32, 128), BF),
            pltpu.VMEM((16, 32, 128), F32),
            pltpu.VMEM((32, 128), F32),
            pltpu.VMEM((2, 32, 64, 128), BF),
            pltpu.SemaphoreType.DMA((7,)),
        ],
        compiler_params=pltpu.CompilerParams(vmem_limit_bytes=60 << 20),
        cost_estimate=pl.CostEstimate(flops=1 << 22, bytes_accessed=3 << 20, transcendentals=0),
    )(acc, pall, irow, istat, qrow, pgain, igain)


def per_device(
    clip_lengths,
    inst_frame,
    query_rows,
    pix_q,
    pix_k,
    pix_v,
    features,
    pixel_gain,
    inst_query,
    inst_gain,
):
    clip_ends = jnp.cumsum(clip_lengths)
    frame_ids = jnp.arange(64, dtype=jnp.int32)
    clip_of = jnp.sum((clip_ends[None, :] <= frame_ids[:, None]).astype(jnp.int32), axis=1)
    same_clip = clip_of[:, None] == clip_of[None, :]
    mask = jnp.where(same_clip, 0.0, MASKED).astype(F32)
    mask = jnp.concatenate([mask, mask], axis=1)
    trow = inst_frame.reshape(1, 128)
    qrow = query_rows.reshape(1, 128)
    inst = inst_query.transpose(1, 2, 0)
    buf, kflat, got = first(pix_q, pix_k, pix_v, inst, trow, qrow)
    buf, got = lax.optimization_barrier((buf, got))
    patch = lax.all_to_all(buf, "st", split_axis=0, concat_axis=0, tiled=True)
    ans, wide = middle(got, kflat, buf, pix_q, pix_k, pix_v, features)
    acc, pall, irow, istat = last(patch, mask, ans, wide, buf, inst, trow)
    pixel_out, inst_out = norm(
        acc, pall, irow, istat, qrow, pixel_gain, inst_gain.reshape(1, 32)
    )
    return pixel_out, inst_out.transpose(2, 0, 1)


def solution(mesh):
    placed = (
        P(),
        P("st", None),
        P("st"),
        P("st", "ha", None, None),
        P("st", "ha", None, None),
        P("st", "ha", None, None),
        P("st", "ha", None, None),
        P("ha"),
        P("st", None, "ha"),
        P("ha"),
    )
    return jax.shard_map(
        per_device,
        mesh=mesh,
        in_specs=placed,
        out_specs=(P("st", "ha", None, None), P("st", None, "ha")),
        check_vma=False,
    )
```
